32 devices in a mesh: roll: 4 (over x, core), mach: 2 (over y), cross: 4 (over z).
Axes of the slice: x: 2, y: 2, z: 4, core: 2. Of those that a mesh axis runs over, the one named last changes fastest.
Arguments:
- density: bfloat16 [128, 4096, 2048], P('roll', 'mach', 'cross'), may hold values from 0 to 1
- roll_start: float32 [32, 128], P(None, 'roll'), may hold values from 0.05 to 1
- mach_factor: bfloat16 [32, 4096], P(None, 'mach'), may hold values from 0.0099487305 to 1
- cross_factor: bfloat16 [32, 2048], P(None, 'cross'), may hold values from 0.0099487305 to 1
Outputs:
- roll_factor: float32 [32, 128], P(None, 'roll')
- mode_two: float32 [32, 4096], P(None, ('mach', 'cross'))
The draws below stay inside these ranges and needn't reach their ends.
All inputs are finite; a program needn't handle non-finite values.
Results may differ from the reference program's by a relative error of at most 0.0003.
Values sent between devices are 32-bit elements; how exact they have to be, the bound alone decides.
No kernel may reach another device: no remote copies, remote signals or barrier semaphores. Data moves between devices by JAX's collectives and lax.ppermute only.
A program may use at most 128 MiB of HBM per device.

```python
import math
import jax
import jax.numpy as jnp
from jax import lax

R = 32
J = 4096
K = 2048
ROLLS = 128


def lognormal_vector(key, count):
    return jnp.exp(jax.random.normal(key, (count,), jnp.float32))


def draw_density(key, part):
    roll_one = lognormal_vector(jax.random.fold_in(key, 11), ROLLS)[:, None, None]
    mach_one = lognormal_vector(jax.random.fold_in(key, 12), J)[None, :, None]
    cross_one = lognormal_vector(jax.random.fold_in(key, 13), K)[None, None, :]
    roll_two = lognormal_vector(jax.random.fold_in(key, 21), ROLLS)[:, None, None]
    mach_two = lognormal_vector(jax.random.fold_in(key, 22), J)[None, :, None]
    cross_two = lognormal_vector(jax.random.fold_in(key, 23), K)[None, None, :]
    noise_key = jax.random.fold_in(key, 31)
    noise = jnp.exp(0.8 * jax.random.normal(noise_key, (ROLLS, J, K), jnp.float32))
    base = roll_one * mach_one * cross_one + roll_two * mach_two * cross_two
    level = 0.25 * base * noise
    return (level / (1.0 + level)).astype(jnp.bfloat16)


def steps_of(stream_key, shape, pieces, smallest, largest):
    level, own = 1.0, jax.random.fold_in(stream_key, 6)
    for position, shards_of in pieces:
        steps = jnp.exp(jax.random.uniform(jax.random.fold_in(own, position), (shards_of,), jnp.float32, smallest / len(pieces), largest / len(pieces)))
        level = level * jnp.repeat(steps, shape[position] // shards_of).reshape([-1 if axis == position else 1 for axis in range(len(shape))])
    return level


def setup_inputs(seed: int = 0) -> dict:
    keys = jax.random.split(jax.random.key(seed), 5)
    density = draw_density(jax.random.fold_in(keys[4], 71), 0)
    roll_start = jnp.clip(jnp.exp(math.log(1.0) - 2.9957323 * jax.random.uniform(keys[1], (R, ROLLS), jnp.float32) ** steps_of(keys[1], (R, ROLLS), ((1, 4),), -0.2, 0.2)), 0.05, 1.0)
    mach_factor = jnp.clip(jnp.exp(math.log(1.0) - 4.61031033 * jax.random.uniform(keys[2], (R, J), jnp.float32) ** steps_of(keys[2], (R, J), ((1, 2),), -0.2, 0.2)), 0.0099487305, 1.0).astype(jnp.bfloat16)
    cross_factor = jnp.clip(jnp.exp(math.log(1.0) - 4.61031033 * jax.random.uniform(keys[3], (R, K), jnp.float32) ** steps_of(keys[3], (R, K), ((1, 4),), -0.2, 0.2)), 0.0099487305, 1.0).astype(jnp.bfloat16)
    return {"density": density, "roll_start": roll_start, "mach_factor": mach_factor, "cross_factor": cross_factor}


def hals_rows(roll_rows, mttkrp, gram):
    def column_step(column, rows):
        column = jnp.asarray(column).astype(jnp.int32)
        gram_row = lax.dynamic_slice_in_dim(gram, column, 1, 0)
        diag_entry = lax.dynamic_slice_in_dim(gram_row, column, 1, 1)
        current = lax.dynamic_slice_in_dim(rows, column, 1, 0)
        target = lax.dynamic_slice_in_dim(mttkrp, column, 1, 0)
        mixed = jnp.dot(gram_row, rows, precision=lax.Precision.HIGHEST)
        updated = jnp.maximum(current + (target - mixed) / diag_entry, 0.0)
        return lax.dynamic_update_slice_in_dim(rows, updated, column, 0)
    return lax.fori_loop(0, roll_rows.shape[0], column_step, roll_rows)


def reference(density, roll_start, mach_factor, cross_factor):
    def one_roll(slab):
        return lax.dot_general(cross_factor, slab, (((1,), (1,)), ((), ())), preferred_element_type=jnp.float32)
    partial_value = lax.map(one_roll, density)
    mttkrp = jnp.einsum('irj,rj->ri', partial_value, mach_factor.astype(jnp.float32), precision=lax.Precision.HIGHEST)
    gram_mach = jnp.dot(mach_factor, mach_factor.T, preferred_element_type=jnp.float32)
    gram_cross = jnp.dot(cross_factor, cross_factor.T, preferred_element_type=jnp.float32)
    gram = gram_mach * gram_cross
    roll_factor = hals_rows(roll_start, mttkrp, gram)
    total = jnp.einsum('irj,ri->rj', partial_value, roll_factor, precision=lax.Precision.HIGHEST)
    scale = R / (ROLLS * K)
    mode_two = total * scale
    return roll_factor, mode_two
```

```python
import functools

import jax
import jax.numpy as jnp
from jax import lax
from jax.experimental import pallas as pl
from jax.experimental.pallas import tpu as pltpu
from jax.sharding import PartitionSpec as P

LANES = 128
MIB = 1024 * 1024


def stream_kernel(
    rolls_per_step, slots, density, mach_hbm, cross_hbm, partial, payload,
    block, mach, cross, weights, spread, terms, sem, factor_sem,
):
    rolls, bins, depth = density.shape
    rank = cross.shape[0]
    groups = LANES // rank
    span = bins // groups
    steps = rolls // rolls_per_step

    def fetch(step, slot):
        return pltpu.make_async_copy(
            density.at[pl.ds(step * rolls_per_step, rolls_per_step)], block.at[slot], sem.at[slot]
        )

    cross_fetch = pltpu.make_async_copy(cross_hbm, cross, factor_sem.at[0])
    mach_fetch = pltpu.make_async_copy(mach_hbm, mach, factor_sem.at[1])
    cross_fetch.start()
    mach_fetch.start()
    for slot in range(slots):
        fetch(slot, slot).start()

    cross_fetch.wait()
    cross_wide = cross[...].astype(jnp.float32)
    cross_lanes = jnp.concatenate([cross_wide] * groups, axis=0).T
    lane_group = lax.broadcasted_iota(jnp.int32, (depth, LANES), 1) // rank
    for group in range(groups):
        weights[group] = jnp.where(lane_group == group, cross_lanes, 0.0).astype(jnp.bfloat16)
    mach_fetch.wait()
    mach_wide = mach[...].astype(jnp.float32)
    spread[...] = jnp.concatenate(
        [mach_wide[:, group * span : (group + 1) * span] for group in range(groups)], axis=0
    ).T

    def one_step(step, carry):
        slot = lax.rem(step, slots)
        fetch(step, slot).wait()
        for part in range(rolls_per_step):
            value = jnp.dot(block[slot, part, 0:span, :], weights[0], preferred_element_type=jnp.float32)
            for group in range(1, groups):
                value = value + jnp.dot(
                    block[slot, part, group * span : (group + 1) * span, :],
                    weights[group],
                    preferred_element_type=jnp.float32,
                )
            roll = step * rolls_per_step + part
            partial[roll] = value
            terms[pl.ds(roll, 1), :] = jnp.sum(value * spread[...], axis=0, keepdims=True)

        @pl.when(step + slots < steps)
        def _():
            fetch(step + slots, slot).start()

        return carry

    lax.fori_loop(0, steps, one_step, 0)

    contract = (((1,), (1,)), ((), ()))
    gram_mach = lax.dot_general(mach[...], mach[...], contract, preferred_element_type=jnp.float32)
    gram_cross = lax.dot_general(cross[...], cross[...], contract, preferred_element_type=jnp.float32)
    summed = terms[:, 0:rank]
    for group in range(1, groups):
        summed = summed + terms[:, group * rank : (group + 1) * rank]
    filler = jnp.zeros((rank, LANES - 3 * rank), jnp.float32)
    payload[...] = jnp.concatenate([summed, gram_mach, gram_cross, filler], axis=1)


def stream(density, mach, cross):
    rolls, bins, depth = density.shape
    rank = cross.shape[0]
    groups = LANES // rank
    span = bins // groups
    rolls_per_step, slots = 2, 4
    in_hbm = functools.partial(pltpu.with_memory_space_constraint, memory_space=pltpu.HBM)
    anywhere = pl.BlockSpec(memory_space=pl.ANY)
    vmem = pl.BlockSpec(memory_space=pltpu.VMEM)
    return pl.pallas_call(
        functools.partial(stream_kernel, rolls_per_step, slots),
        out_shape=(
            pltpu.VMEM((rolls, span, LANES), jnp.float32),
            pltpu.VMEM((rolls, LANES), jnp.float32),
        ),
        in_specs=[anywhere, anywhere, anywhere],
        out_specs=(vmem, vmem),
        scratch_shapes=[
            pltpu.VMEM((slots, rolls_per_step, bins, depth), jnp.bfloat16),
            pltpu.VMEM(mach.shape, mach.dtype),
            pltpu.VMEM(cross.shape, cross.dtype),
            pltpu.VMEM((groups, depth, LANES), jnp.bfloat16),
            pltpu.VMEM((span, LANES), jnp.float32),
            pltpu.VMEM((rolls, LANES), jnp.float32),
            pltpu.SemaphoreType.DMA((slots,)),
            pltpu.SemaphoreType.DMA((2,)),
        ],
        compiler_params=pltpu.CompilerParams(vmem_limit_bytes=40 * MIB),
        cost_estimate=pl.CostEstimate(
            flops=2 * rolls * bins * depth * rank, bytes_accessed=2 * rolls * bins * depth, transcendentals=0
        ),
        name="stream",
    )(density, in_hbm(mach), in_hbm(cross))


def update_kernel(scale, place, partial, payload, start, roll_out, keep, send, total, roll_rows, sem):
    rolls, span, lanes = partial.shape
    rank = start.shape[0]
    groups = lanes // rank
    half = rank // 2
    flipped = payload[...].T
    gram = flipped[rank : 2 * rank] * flipped[2 * rank : 3 * rank]
    row_id = lax.broadcasted_iota(jnp.int32, (rank, rank), 0)
    lane_id = lax.broadcasted_iota(jnp.int32, (rank, rank), 1)
    diag = jnp.sum(jnp.where(row_id == lane_id, gram, 0.0), axis=1, keepdims=True)
    share = gram / diag
    rows = start[...]
    gap = flipped[0:rank] / diag
    for r in range(rank):
        gap = gap - share[:, r : r + 1] * rows[r : r + 1, :]
    done = []
    for r in range(rank):
        current = rows[r : r + 1, :]
        updated = jnp.maximum(current + gap[r : r + 1, :], 0.0)
        gap = gap - share[:, r : r + 1] * (updated - current)
        done.append(updated)
    factor = jnp.concatenate(done, axis=0)
    roll_rows[...] = factor
    store = pltpu.make_async_copy(roll_rows, roll_out, sem)
    store.start()
    factor_lanes = jnp.concatenate([factor * scale] * groups, axis=0).T

    chunk = min(span, 64)
    for first in range(0, span, chunk):
        value = partial[0, first : first + chunk, :] * factor_lanes[0:1, :]
        for roll in range(1, rolls):
            value = value + partial[roll, first : first + chunk, :] * factor_lanes[roll : roll + 1, :]
        total[first : first + chunk, :] = value
    blocks = total[...].T.reshape(groups, 2, half, span)
    core = place[0]
    cross_at = place[1]
    low_first = (0, 2, 1, 3)
    for slot, distance in enumerate(low_first):
        for group in range(groups):

            @pl.when(cross_at ^ distance == group)
            def _():
                @pl.when(core == 0)
                def _():
                    keep[slot] = blocks[group, 0]
                    send[slot] = blocks[group, 1]

                @pl.when(core != 0)
                def _():
                    keep[slot] = blocks[group, 1]
                    send[slot] = blocks[group, 0]

    store.wait()


def update(scale, place, partial, payload, start):
    rolls, span, lanes = partial.shape
    rank = start.shape[0]
    groups = lanes // rank
    vmem = pl.BlockSpec(memory_space=pltpu.VMEM)
    part = pltpu.VMEM((groups, rank // 2, span), jnp.float32)
    return pl.pallas_call(
        functools.partial(update_kernel, scale),
        out_shape=(jax.ShapeDtypeStruct((rank, rolls), jnp.float32), part, part),
        in_specs=[pl.BlockSpec(memory_space=pltpu.SMEM), vmem, vmem, vmem],
        out_specs=(pl.BlockSpec(memory_space=pl.ANY), vmem, vmem),
        scratch_shapes=[
            pltpu.VMEM((span, lanes), jnp.float32),
            pltpu.VMEM((rank, rolls), jnp.float32),
            pltpu.SemaphoreType.DMA,
        ],
        compiler_params=pltpu.CompilerParams(vmem_limit_bytes=40 * MIB),
        cost_estimate=pl.CostEstimate(flops=4 * rolls * span * lanes, bytes_accessed=0, transcendentals=0),
        name="update",
    )(place, pltpu.with_memory_space_constraint(partial, pltpu.VMEM), payload, start)


def swap(value, axes, distance):
    axes = axes if isinstance(axes, tuple) else (axes,)
    count = 1
    for axis in axes:
        count *= lax.axis_size(axis)
    return lax.ppermute(value, axes, [(source, source ^ distance) for source in range(count)])


def reduce_payload(payload, rank):
    mach_size, cross_size = lax.axis_size("mach"), lax.axis_size("cross")
    lane = lax.broadcasted_iota(jnp.int32, payload.shape, 1)
    is_term = lane < rank
    is_mach = jnp.logical_and(lane >= rank, lane < 2 * rank)
    is_cross = jnp.logical_and(lane >= 2 * rank, lane < 3 * rank)

    both = ("mach", "cross")
    over_mach = swap(payload, both, cross_size)
    over_cross = swap(payload, both, 1)
    over_both = swap(payload, both, cross_size + 1)
    payload = payload + (
        jnp.where(jnp.logical_or(is_term, is_mach), over_mach, 0.0)
        + jnp.where(jnp.logical_or(is_term, is_cross), over_cross, 0.0)
        + jnp.where(is_term, over_both, 0.0)
    )
    distance = 2
    while distance < mach_size:
        arrived = swap(payload, "mach", distance)
        payload = payload + jnp.where(is_cross, 0.0, arrived)
        distance *= 2
    distance = 2
    while distance < cross_size:
        arrived = swap(payload, "cross", distance)
        payload = payload + jnp.where(is_mach, 0.0, arrived)
        distance *= 2
    return payload


def reduce_blocks(keep, send):
    cross_size = lax.axis_size("cross")
    value = keep + swap(send, "roll", 1)
    mine, his = value[:2], value[2:]
    by_cross = swap(his, "cross", 1)
    by_roll = swap(mine, "roll", 2)
    by_both = swap(his, ("roll", "cross"), 2 * cross_size + 1)
    value = mine + (by_cross + (by_roll + by_both))
    value = value[0] + swap(value[1], "cross", 2)
    other = swap(value, "roll", 1)
    core = lax.axis_index("roll") % 2
    return jnp.where(
        core == 0, jnp.concatenate([value, other], axis=0), jnp.concatenate([other, value], axis=0)
    )


def local(density, roll_start, mach_factor, cross_factor):
    rolls_here, _, cross_here = density.shape
    rank = cross_factor.shape[0]
    all_rolls = rolls_here * lax.axis_size("roll")
    all_cross = cross_here * lax.axis_size("cross")
    scale = rank / (all_rolls * all_cross)
    place = jnp.stack([lax.axis_index("roll") % 2, lax.axis_index("cross")]).astype(jnp.int32)
    partial_value, payload = stream(density, mach_factor, cross_factor)
    payload = reduce_payload(payload, rank)
    roll_factor, keep, send = update(scale, place, partial_value, payload, roll_start)
    return (roll_factor, reduce_blocks(keep, send))


def solution(mesh):
    assert mesh.shape["roll"] == 4 and mesh.shape["cross"] == 4
    in_specs = (P("roll", "mach", "cross"), P(None, "roll"), P(None, "mach"), P(None, "cross"))
    out_specs = (P(None, "roll"), P(None, ("mach", "cross")))
    return jax.shard_map(local, mesh=mesh, in_specs=in_specs, out_specs=out_specs, check_vma=False)
```

```python
import functools

import jax
import jax.numpy as jnp
from jax import lax
from jax.experimental import pallas as pl
from jax.experimental.pallas import tpu as pltpu
from jax.sharding import PartitionSpec as P

LANES = 128
MIB = 1024 * 1024


def stream_kernel(
    rolls_per_step, slots, ahead, density, mach_hbm, cross_hbm, partial, payload,
    block, mach, cross, weights, spread, terms, sem, factor_sem,
):
    rolls, bins, depth = density.shape
    rank = cross.shape[0]
    groups = LANES // rank
    span = bins // groups
    steps = rolls // rolls_per_step

    def fetch(step, slot):
        return pltpu.make_async_copy(
            density.at[pl.ds(step * rolls_per_step, rolls_per_step)], block.at[slot], sem.at[slot]
        )

    cross_fetch = pltpu.make_async_copy(cross_hbm, cross, factor_sem.at[0])
    mach_fetch = pltpu.make_async_copy(mach_hbm, mach, factor_sem.at[1])
    cross_fetch.start()
    mach_fetch.start()
    for slot in range(ahead):
        fetch(slot, slot).start()

    cross_fetch.wait()
    cross_wide = cross[...].astype(jnp.float32)
    cross_lanes = jnp.concatenate([cross_wide] * groups, axis=0).T
    lane_group = lax.broadcasted_iota(jnp.int32, (depth, LANES), 1) // rank
    for group in range(groups):
        weights[group] = jnp.where(lane_group == group, cross_lanes, 0.0).astype(jnp.bfloat16)
    mach_fetch.wait()
    mach_wide = mach[...].astype(jnp.float32)
    spread[...] = jnp.concatenate(
        [mach_wide[:, group * span : (group + 1) * span] for group in range(groups)], axis=0
    ).T

    def one_step(step, carry):
        slot = lax.rem(step, slots)

        @pl.when(step + ahead < steps)
        def _():
            fetch(step + ahead, lax.rem(step + ahead, slots)).start()

        fetch(step, slot).wait()
        for part in range(rolls_per_step):
            value = jnp.dot(block[slot, part, 0:span, :], weights[0], preferred_element_type=jnp.float32)
            for group in range(1, groups):
                value = value + jnp.dot(
                    block[slot, part, group * span : (group + 1) * span, :],
                    weights[group],
                    preferred_element_type=jnp.float32,
                )
            roll = step * rolls_per_step + part
            partial[roll] = value
            terms[pl.ds(roll, 1), :] = jnp.sum(value * spread[...], axis=0, keepdims=True)
        return carry

    lax.fori_loop(0, steps, one_step, 0)

    contract = (((1,), (1,)), ((), ()))
    gram_mach = lax.dot_general(mach[...], mach[...], contract, preferred_element_type=jnp.float32)
    gram_cross = lax.dot_general(cross[...], cross[...], contract, preferred_element_type=jnp.float32)
    summed = terms[:, 0:rank]
    for group in range(1, groups):
        summed = summed + terms[:, group * rank : (group + 1) * rank]
    filler = jnp.zeros((rank, LANES - 3 * rank), jnp.float32)
    payload[...] = jnp.concatenate([summed, gram_mach, gram_cross, filler], axis=1)


def stream(density, mach, cross):
    rolls, bins, depth = density.shape
    rank = cross.shape[0]
    groups = LANES // rank
    span = bins // groups
    rolls_per_step, slots, ahead = 2, 4, 2
    in_hbm = functools.partial(pltpu.with_memory_space_constraint, memory_space=pltpu.HBM)
    anywhere = pl.BlockSpec(memory_space=pl.ANY)
    vmem = pl.BlockSpec(memory_space=pltpu.VMEM)
    return pl.pallas_call(
        functools.partial(stream_kernel, rolls_per_step, slots, ahead),
        out_shape=(
            pltpu.VMEM((rolls, span, LANES), jnp.float32),
            pltpu.VMEM((rolls, LANES), jnp.float32),
        ),
        in_specs=[anywhere, anywhere, anywhere],
        out_specs=(vmem, vmem),
        scratch_shapes=[
            pltpu.VMEM((slots, rolls_per_step, bins, depth), jnp.bfloat16),
            pltpu.VMEM(mach.shape, mach.dtype),
            pltpu.VMEM(cross.shape, cross.dtype),
            pltpu.VMEM((groups, depth, LANES), jnp.bfloat16),
            pltpu.VMEM((span, LANES), jnp.float32),
            pltpu.VMEM((rolls, LANES), jnp.float32),
            pltpu.SemaphoreType.DMA((slots,)),
            pltpu.SemaphoreType.DMA((2,)),
        ],
        compiler_params=pltpu.CompilerParams(vmem_limit_bytes=40 * MIB),
        cost_estimate=pl.CostEstimate(
            flops=2 * rolls * bins * depth * rank, bytes_accessed=2 * rolls * bins * depth, transcendentals=0
        ),
        name="stream",
    )(density, in_hbm(mach), in_hbm(cross))


def update_kernel(scale, partial, payload, start, roll_out, keep, send, total, blocks, roll_rows, sem):
    rolls, span, lanes = partial.shape
    rank = start.shape[0]
    groups = lanes // rank
    half = rank // 2
    flipped = payload[...].T
    gram = flipped[rank : 2 * rank] * flipped[2 * rank : 3 * rank]
    row_id = lax.broadcasted_iota(jnp.int32, (rank, rank), 0)
    lane_id = lax.broadcasted_iota(jnp.int32, (rank, rank), 1)
    diag = jnp.sum(jnp.where(row_id == lane_id, gram, 0.0), axis=1, keepdims=True)
    share = gram / diag
    rows = start[...]
    gap = flipped[0:rank] / diag
    for r in range(rank):
        gap = gap - share[:, r : r + 1] * rows[r : r + 1, :]
    done = []
    for r in range(rank):
        current = rows[r : r + 1, :]
        updated = jnp.maximum(current + gap[r : r + 1, :], 0.0)
        gap = gap - share[:, r : r + 1] * (updated - current)
        done.append(updated)
    factor = jnp.concatenate(done, axis=0)
    roll_rows[...] = factor
    store = pltpu.make_async_copy(roll_rows, roll_out, sem)
    store.start()
    factor_lanes = jnp.concatenate([factor * scale] * groups, axis=0).T

    chunk = min(span, 64)
    for first in range(0, span, chunk):
        value = partial[0, first : first + chunk, :] * factor_lanes[0:1, :]
        for roll in range(1, rolls):
            value = value + partial[roll, first : first + chunk, :] * factor_lanes[roll : roll + 1, :]
        total[first : first + chunk, :] = value
    blocks[...] = total[...].T.reshape(groups, 2, half, span)
    core = lax.rem(lax.axis_index("roll"), 2)
    cross_at = lax.axis_index("cross")
    for slot, distance in enumerate((0, 2, 1, 3)):
        keep[slot] = blocks[cross_at ^ distance, core]
        send[slot] = blocks[cross_at ^ distance, 1 - core]
    store.wait()


def update(scale, partial, payload, start):
    rolls, span, lanes = partial.shape
    rank = start.shape[0]
    groups = lanes // rank
    vmem = pl.BlockSpec(memory_space=pltpu.VMEM)
    part = pltpu.VMEM((groups, rank // 2, span), jnp.float32)
    return pl.pallas_call(
        functools.partial(update_kernel, scale),
        out_shape=(jax.ShapeDtypeStruct((rank, rolls), jnp.float32), part, part),
        in_specs=[vmem, vmem, vmem],
        out_specs=(pl.BlockSpec(memory_space=pl.ANY), vmem, vmem),
        scratch_shapes=[
            pltpu.VMEM((span, lanes), jnp.float32),
            pltpu.VMEM((groups, 2, rank // 2, span), jnp.float32),
            pltpu.VMEM((rank, rolls), jnp.float32),
            pltpu.SemaphoreType.DMA,
        ],
        compiler_params=pltpu.CompilerParams(vmem_limit_bytes=40 * MIB),
        cost_estimate=pl.CostEstimate(flops=4 * rolls * span * lanes, bytes_accessed=0, transcendentals=0),
        name="update",
    )(pltpu.with_memory_space_constraint(partial, pltpu.VMEM), payload, start)


def swap(value, axes, distance):
    axes = axes if isinstance(axes, tuple) else (axes,)
    count = 1
    for axis in axes:
        count *= lax.axis_size(axis)
    return lax.ppermute(value, axes, [(source, source ^ distance) for source in range(count)])


def reduce_payload(payload, rank):
    mach_size, cross_size = lax.axis_size("mach"), lax.axis_size("cross")
    lane = lax.broadcasted_iota(jnp.int32, payload.shape, 1)
    is_term = lane < rank
    is_mach = jnp.logical_and(lane >= rank, lane < 2 * rank)
    is_cross = jnp.logical_and(lane >= 2 * rank, lane < 3 * rank)

    both = ("mach", "cross")
    over_mach = swap(payload, both, cross_size)
    over_cross = swap(payload, both, 1)
    over_both = swap(payload, both, cross_size + 1)
    payload = payload + (
        jnp.where(jnp.logical_or(is_term, is_mach), over_mach, 0.0)
        + jnp.where(jnp.logical_or(is_term, is_cross), over_cross, 0.0)
        + jnp.where(is_term, over_both, 0.0)
    )
    distance = 2
    while distance < mach_size:
        arrived = swap(payload, "mach", distance)
        payload = payload + jnp.where(is_cross, 0.0, arrived)
        distance *= 2
    distance = 2
    while distance < cross_size:
        arrived = swap(payload, "cross", distance)
        payload = payload + jnp.where(is_mach, 0.0, arrived)
        distance *= 2
    return payload


def reduce_blocks(keep, send):
    cross_size = lax.axis_size("cross")
    value = keep + swap(send, "roll", 1)
    mine, his = value[:2], value[2:]
    by_cross = swap(his, "cross", 1)
    by_roll = swap(mine, "roll", 2)
    by_both = swap(his, ("roll", "cross"), 2 * cross_size + 1)
    value = mine + (by_cross + (by_roll + by_both))
    value = value[0] + swap(value[1], "cross", 2)
    return join(value, swap(value, "roll", 1))


def join_kernel(own, other, out, sem):
    core = lax.rem(lax.axis_index("roll"), 2)
    half = own.shape[0]
    first = pltpu.make_async_copy(own, out.at[pl.ds(pl.multiple_of(core * half, half), half)], sem.at[0])
    second = pltpu.make_async_copy(other, out.at[pl.ds(pl.multiple_of((1 - core) * half, half), half)], sem.at[1])
    first.start()
    second.start()
    first.wait()
    second.wait()


def join(own, other):
    vmem = pl.BlockSpec(memory_space=pltpu.VMEM)
    return pl.pallas_call(
        join_kernel,
        out_shape=jax.ShapeDtypeStruct((2 * own.shape[0], own.shape[1]), own.dtype),
        in_specs=[vmem, vmem],
        out_specs=pl.BlockSpec(memory_space=pl.ANY),
        scratch_shapes=[pltpu.SemaphoreType.DMA((2,))],
        compiler_params=pltpu.CompilerParams(vmem_limit_bytes=8 * MIB),
        name="join",
    )(own, other)


def local(density, roll_start, mach_factor, cross_factor):
    rolls_here, _, cross_here = density.shape
    rank = cross_factor.shape[0]
    all_rolls = rolls_here * lax.axis_size("roll")
    all_cross = cross_here * lax.axis_size("cross")
    scale = rank / (all_rolls * all_cross)
    partial_value, payload = stream(density, mach_factor, cross_factor)
    payload = reduce_payload(payload, rank)
    roll_factor, keep, send = update(scale, partial_value, payload, roll_start)
    return (roll_factor, reduce_blocks(keep, send))


def solution(mesh):
    assert mesh.shape["roll"] == 4 and mesh.shape["cross"] == 4
    in_specs = (P("roll", "mach", "cross"), P(None, "roll"), P(None, "mach"), P(None, "cross"))
    out_specs = (P(None, "roll"), P(None, ("mach", "cross")))
    return jax.shard_map(local, mesh=mesh, in_specs=in_specs, out_specs=out_specs, check_vma=False)
```

```python
import functools

import jax
import jax.numpy as jnp
from jax import lax
from jax.experimental import pallas as pl
from jax.experimental.pallas import tpu as pltpu
from jax.sharding import PartitionSpec as P

LANES = 128
MIB = 1024 * 1024
WIDE = 256
UNITS = 2


def stream_kernel(
    density, mach_hbm, cross_hbm, partial, payload,
    block, mach, cross, weights, spread, terms, mach_rows, cross_rows, grams, sem, factor_sem,
):
    rolls, bins, depth = density.shape
    rank = cross.shape[0]
    groups = LANES // rank
    span = bins // groups
    slots = block.shape[0]
    ahead = 4
    tiles = 2 * groups
    tile_rows = span // 2
    part_rows = min(tile_rows, 128)
    parts = tile_rows // part_rows

    def fetch(roll, slot):
        return pltpu.make_async_copy(density.at[roll], block.at[slot], sem.at[slot])

    cross_fetch = pltpu.make_async_copy(cross_hbm, cross, factor_sem.at[0])
    mach_fetch = pltpu.make_async_copy(mach_hbm, mach, factor_sem.at[1])
    cross_fetch.start()
    mach_fetch.start()
    fetch(0, 0).start()

    def multiply(*sums):
        turns, gram_sums = sums[:-UNITS], sums[-UNITS:]

        def sum_of(turn, unit, part):
            return turns[(turn * UNITS + unit) * parts + part]

        def issue(turn, slot, tile):
            for unit in range(UNITS):
                pltpu.matmul_push_rhs(weights[tile, unit * WIDE : (unit + 1) * WIDE, :], tile % 2, unit)
            for part in range(parts):
                first = tile * tile_rows + part * part_rows
                for unit in range(UNITS):
                    pltpu.matmul_acc_lhs(
                        sum_of(turn, unit, part),
                        block[slot, first : first + part_rows, unit * WIDE : (unit + 1) * WIDE],
                        load_staged_rhs=tile % 2 if part == 0 else None,
                    )

        def collect(turn, roll, part):
            value = pltpu.matmul_pop(sum_of(turn, 0, part)) + pltpu.matmul_pop(sum_of(turn, 1, part))
            total = None
            for half in range(2):
                first = half * tile_rows + part * part_rows
                piece = value[:, half * LANES : (half + 1) * LANES]
                partial[roll, first : first + part_rows, :] = piece
                weighted = piece * spread[first : first + part_rows, :]
                total = weighted if total is None else total + weighted
            return jnp.sum(total, axis=0, keepdims=True)

        def finish(roll, pieces):
            terms[pl.ds(roll, 1), :] = sum(pieces[1:], pieces[0])

        def one_roll(turn, slot, roll_before):
            pieces = []
            for tile in range(tiles):
                issue(turn, slot, tile)
                for part in range(tile * parts // tiles, (tile + 1) * parts // tiles):
                    pieces.append(collect(1 - turn, roll_before, part))
            finish(roll_before, pieces)

        cross_fetch.wait()
        fetch(1, 1).start()
        fetch(2, 2).start()
        cross_lanes = jnp.concatenate([cross[...].astype(jnp.float32)] * groups, axis=0).T
        lane_group = lax.broadcasted_iota(jnp.int32, (depth, LANES), 1) // rank
        blank = jnp.zeros((depth, LANES), jnp.bfloat16)
        for tile in range(tiles):
            near, far = tile % 2 * LANES, (1 - tile % 2) * LANES
            placed = jnp.where(lane_group == tile // 2, cross_lanes, 0.0).astype(jnp.bfloat16)
            weights[tile, :, near : near + LANES] = placed
            weights[tile, :, far : far + LANES] = blank
        mach_fetch.wait()
        fetch(3, 3).start()
        spread[...] = jnp.concatenate(
            [mach[:, group * span : (group + 1) * span].astype(jnp.float32) for group in range(groups)], axis=0
        ).T

        for part in range(parts):
            collect(0, 0, part)
        for unit in range(UNITS):
            pltpu.matmul_pop(gram_sums[unit])

        mach_rows[...] = jnp.zeros_like(mach_rows)
        mach_rows[rank : 2 * rank, :] = mach[...]
        cross_rows[...] = jnp.zeros_like(cross_rows)
        cross_rows[2 * rank : 3 * rank, :] = cross[...]
        work = [(mach_rows, mach, first) for first in range(0, bins, WIDE)]
        work += [(cross_rows, cross, first) for first in range(0, depth, WIDE)]
        for count, (right, left, first) in enumerate(work):
            unit, stage = count % UNITS, count // UNITS % 2
            pltpu.matmul_push_rhs(right[:, first : first + WIDE], stage, unit, transpose=True)
            pltpu.matmul_acc_lhs(gram_sums[unit], left[:, first : first + WIDE], load_staged_rhs=stage)
        grams[...] = (pltpu.matmul_pop(gram_sums[0]) + pltpu.matmul_pop(gram_sums[1]))[:, 0:LANES]

        def two_rolls(step, carry):
            roll = 2 * step
            slot = lax.rem(roll, slots)

            @pl.when(roll + ahead < rolls)
            def _():
                next_slot = lax.rem(roll + ahead, slots)
                fetch(roll + ahead, next_slot).start()
                fetch(roll + ahead + 1, next_slot + 1).start()

            fetch(roll, slot).wait()
            one_roll(0, slot, jnp.maximum(roll - 1, 0))
            fetch(roll + 1, slot + 1).wait()
            one_roll(1, slot + 1, roll)
            return carry

        lax.fori_loop(0, rolls // 2, two_rolls, 0)
        finish(rolls - 1, [collect(1, rolls - 1, part) for part in range(parts)])

    pl.run_scoped(
        multiply,
        *[pltpu.ACC(unit)((part_rows, WIDE), jnp.float32) for _ in range(2) for unit in range(UNITS) for _ in range(parts)],
        *[pltpu.ACC(unit)((rank, WIDE), jnp.float32) for unit in range(UNITS)],
    )

    summed = terms[:, 0:rank]
    for group in range(1, groups):
        summed = summed + terms[:, group * rank : (group + 1) * rank]
    payload[...] = grams[...]
    payload[:, 0:rank] = summed


def stream(density, mach, cross):
    rolls, bins, depth = density.shape
    rank = cross.shape[0]
    groups = LANES // rank
    span = bins // groups
    slots = 8
    assert rolls == rank and depth == UNITS * WIDE
    in_hbm = functools.partial(pltpu.with_memory_space_constraint, memory_space=pltpu.HBM)
    anywhere = pl.BlockSpec(memory_space=pl.ANY)
    vmem = pl.BlockSpec(memory_space=pltpu.VMEM)
    return pl.pallas_call(
        stream_kernel,
        out_shape=(
            pltpu.VMEM((rolls, span, LANES), jnp.float32),
            pltpu.VMEM((rolls, LANES), jnp.float32),
        ),
        in_specs=[anywhere, anywhere, anywhere],
        out_specs=(vmem, vmem),
        scratch_shapes=[
            pltpu.VMEM((slots, bins, depth), jnp.bfloat16),
            pltpu.VMEM(mach.shape, mach.dtype),
            pltpu.VMEM(cross.shape, cross.dtype),
            pltpu.VMEM((2 * groups, depth, WIDE), jnp.bfloat16),
            pltpu.VMEM((span, LANES), jnp.float32),
            pltpu.VMEM((rolls, LANES), jnp.float32),
            pltpu.VMEM((WIDE, bins), jnp.bfloat16),
            pltpu.VMEM((WIDE, depth), jnp.bfloat16),
            pltpu.VMEM((rank, LANES), jnp.float32),
            pltpu.SemaphoreType.DMA((slots,)),
            pltpu.SemaphoreType.DMA((2,)),
        ],
        compiler_params=pltpu.CompilerParams(vmem_limit_bytes=40 * MIB),
        cost_estimate=pl.CostEstimate(
            flops=2 * rolls * bins * depth * rank, bytes_accessed=2 * rolls * bins * depth, transcendentals=0
        ),
        name="stream",
    )(density, in_hbm(mach), in_hbm(cross))


def update_kernel(scale, partial, payload, start, roll_out, keep, send, total, blocks, roll_rows, sem):
    rolls, span, lanes = partial.shape
    rank = start.shape[0]
    groups = lanes // rank
    half = rank // 2
    flipped = payload[...].T
    gram = flipped[rank : 2 * rank] * flipped[2 * rank : 3 * rank]
    row_id = lax.broadcasted_iota(jnp.int32, (rank, rank), 0)
    lane_id = lax.broadcasted_iota(jnp.int32, (rank, rank), 1)
    diag = jnp.sum(jnp.where(row_id == lane_id, gram, 0.0), axis=1, keepdims=True)
    share = gram / diag
    rows = start[...]
    gap = flipped[0:rank] / diag
    for r in range(rank):
        gap = gap - share[:, r : r + 1] * rows[r : r + 1, :]
    done = []
    for r in range(rank):
        current = rows[r : r + 1, :]
        updated = jnp.maximum(current + gap[r : r + 1, :], 0.0)
        gap = gap - share[:, r : r + 1] * (updated - current)
        done.append(updated)
    factor = jnp.concatenate(done, axis=0)
    roll_rows[...] = factor
    store = pltpu.make_async_copy(roll_rows, roll_out, sem)
    store.start()
    factor_lanes = jnp.concatenate([factor * scale] * groups, axis=0).T

    chunk = min(span, 64)
    for first in range(0, span, chunk):
        value = partial[0, first : first + chunk, :] * factor_lanes[0:1, :]
        for roll in range(1, rolls):
            value = value + partial[roll, first : first + chunk, :] * factor_lanes[roll : roll + 1, :]
        total[first : first + chunk, :] = value
    blocks[...] = total[...].T.reshape(groups, 2, half, span)
    core = lax.rem(lax.axis_index("roll"), 2)
    cross_at = lax.axis_index("cross")
    for slot, distance in enumerate((0, 2, 1, 3)):
        keep[slot] = blocks[cross_at ^ distance, core]
        send[slot] = blocks[cross_at ^ distance, 1 - core]
    store.wait()


def update(scale, partial, payload, start):
    rolls, span, lanes = partial.shape
    rank = start.shape[0]
    groups = lanes // rank
    vmem = pl.BlockSpec(memory_space=pltpu.VMEM)
    part = pltpu.VMEM((groups, rank // 2, span), jnp.float32)
    return pl.pallas_call(
        functools.partial(update_kernel, scale),
        out_shape=(jax.ShapeDtypeStruct((rank, rolls), jnp.float32), part, part),
        in_specs=[vmem, vmem, vmem],
        out_specs=(pl.BlockSpec(memory_space=pl.ANY), vmem, vmem),
        scratch_shapes=[
            pltpu.VMEM((span, lanes), jnp.float32),
            pltpu.VMEM((groups, 2, rank // 2, span), jnp.float32),
            pltpu.VMEM((rank, rolls), jnp.float32),
            pltpu.SemaphoreType.DMA,
        ],
        compiler_params=pltpu.CompilerParams(vmem_limit_bytes=40 * MIB),
        cost_estimate=pl.CostEstimate(flops=4 * rolls * span * lanes, bytes_accessed=0, transcendentals=0),
        name="update",
    )(pltpu.with_memory_space_constraint(partial, pltpu.VMEM), payload, start)


def swap(value, axes, distance):
    axes = axes if isinstance(axes, tuple) else (axes,)
    count = 1
    for axis in axes:
        count *= lax.axis_size(axis)
    return lax.ppermute(value, axes, [(source, source ^ distance) for source in range(count)])


def reduce_payload(payload, rank):
    mach_size, cross_size = lax.axis_size("mach"), lax.axis_size("cross")
    lane = lax.broadcasted_iota(jnp.int32, payload.shape, 1)
    is_term = lane < rank
    is_mach = jnp.logical_and(lane >= rank, lane < 2 * rank)
    is_cross = jnp.logical_and(lane >= 2 * rank, lane < 3 * rank)

    both = ("mach", "cross")
    over_mach = swap(payload, both, cross_size)
    over_cross = swap(payload, both, 1)
    over_both = swap(payload, both, cross_size + 1)
    payload = payload + (
        jnp.where(jnp.logical_or(is_term, is_mach), over_mach, 0.0)
        + jnp.where(jnp.logical_or(is_term, is_cross), over_cross, 0.0)
        + jnp.where(is_term, over_both, 0.0)
    )
    distance = 2
    while distance < mach_size:
        arrived = swap(payload, "mach", distance)
        payload = payload + jnp.where(is_cross, 0.0, arrived)
        distance *= 2
    distance = 2
    while distance < cross_size:
        arrived = swap(payload, "cross", distance)
        payload = payload + jnp.where(is_mach, 0.0, arrived)
        distance *= 2
    return payload


def reduce_blocks(keep, send):
    cross_size = lax.axis_size("cross")
    value = keep + swap(send, "roll", 1)
    mine, his = value[:2], value[2:]
    by_cross = swap(his, "cross", 1)
    by_roll = swap(mine, "roll", 2)
    by_both = swap(his, ("roll", "cross"), 2 * cross_size + 1)
    value = mine + (by_cross + (by_roll + by_both))
    value = value[0] + swap(value[1], "cross", 2)
    return join(value, swap(value, "roll", 1))


def join_kernel(own, other, out, sem):
    core = lax.rem(lax.axis_index("roll"), 2)
    half = own.shape[0]
    first = pltpu.make_async_copy(own, out.at[pl.ds(pl.multiple_of(core * half, half), half)], sem.at[0])
    second = pltpu.make_async_copy(other, out.at[pl.ds(pl.multiple_of((1 - core) * half, half), half)], sem.at[1])
    first.start()
    second.start()
    first.wait()
    second.wait()


def join(own, other):
    vmem = pl.BlockSpec(memory_space=pltpu.VMEM)
    return pl.pallas_call(
        join_kernel,
        out_shape=jax.ShapeDtypeStruct((2 * own.shape[0], own.shape[1]), own.dtype),
        in_specs=[vmem, vmem],
        out_specs=pl.BlockSpec(memory_space=pl.ANY),
        scratch_shapes=[pltpu.SemaphoreType.DMA((2,))],
        compiler_params=pltpu.CompilerParams(vmem_limit_bytes=8 * MIB),
        name="join",
    )(own, other)


def local(density, roll_start, mach_factor, cross_factor):
    rolls_here, _, cross_here = density.shape
    rank = cross_factor.shape[0]
    all_rolls = rolls_here * lax.axis_size("roll")
    all_cross = cross_here * lax.axis_size("cross")
    scale = rank / (all_rolls * all_cross)
    partial_value, payload = stream(density, mach_factor, cross_factor)
    payload = reduce_payload(payload, rank)
    roll_factor, keep, send = update(scale, partial_value, payload, roll_start)
    return (roll_factor, reduce_blocks(keep, send))


def solution(mesh):
    assert mesh.shape["roll"] == 4 and mesh.shape["cross"] == 4
    in_specs = (P("roll", "mach", "cross"), P(None, "roll"), P(None, "mach"), P(None, "cross"))
    out_specs = (P(None, "roll"), P(None, ("mach", "cross")))
    return jax.shard_map(local, mesh=mesh, in_specs=in_specs, out_specs=out_specs, check_vma=False)
```

```python
import functools

import jax
import jax.numpy as jnp
from jax import lax
from jax.experimental import pallas as pl
from jax.experimental.pallas import tpu as pltpu
from jax.sharding import PartitionSpec as P

LANES = 128
MIB = 1024 * 1024
WIDE = 256
UNITS = 2


def stream_kernel(
    density, mach_hbm, cross_hbm, partial, payload,
    block, mach, cross, weights, spread, terms, mach_rows, cross_rows, grams, sem, factor_sem,
):
    rolls, bins, depth = density.shape
    rank = cross.shape[0]
    groups = LANES // rank
    span = bins // groups
    slots = block.shape[0]
    ahead = 4
    tiles = 2 * groups
    tile_rows = span // 2
    part_rows = min(tile_rows, 128)
    parts = tile_rows // part_rows

    def fetch(roll, slot):
        return pltpu.make_async_copy(density.at[roll], block.at[slot], sem.at[slot])

    cross_fetch = pltpu.make_async_copy(cross_hbm, cross, factor_sem.at[0])
    mach_fetch = pltpu.make_async_copy(mach_hbm, mach, factor_sem.at[1])
    cross_fetch.start()
    mach_fetch.start()
    fetch(0, 0).start()

    def multiply(*sums):
        turns, gram_sums = sums[:-UNITS], sums[-UNITS:]

        def sum_of(turn, unit, part):
            return turns[(turn * UNITS + unit) * parts + part]

        def issue(turn, slot, tile):
            for unit in range(UNITS):
                pltpu.matmul_push_rhs(weights[tile, unit * WIDE : (unit + 1) * WIDE, :], tile % 2, unit)
            for part in range(parts):
                first = tile * tile_rows + part * part_rows
                for unit in range(UNITS):
                    pltpu.matmul_acc_lhs(
                        sum_of(turn, unit, part),
                        block[slot, first : first + part_rows, unit * WIDE : (unit + 1) * WIDE],
                        load_staged_rhs=tile % 2 if part == 0 else None,
                    )

        def collect(turn, roll, part):
            value = pltpu.matmul_pop(sum_of(turn, 0, part)) + pltpu.matmul_pop(sum_of(turn, 1, part))
            total = None
            for half in range(2):
                first = half * tile_rows + part * part_rows
                piece = value[:, half * LANES : (half + 1) * LANES]
                partial[roll, first : first + part_rows, :] = piece
                weighted = piece * spread[first : first + part_rows, :]
                total = weighted if total is None else total + weighted
            return jnp.sum(total, axis=0, keepdims=True)

        def finish(roll, pieces):
            terms[pl.ds(roll, 1), :] = sum(pieces[1:], pieces[0])

        def one_roll(turn, slot, roll_before):
            pieces = []
            for tile in range(tiles):
                issue(turn, slot, tile)
                for part in range(tile * parts // tiles, (tile + 1) * parts // tiles):
                    pieces.append(collect(1 - turn, roll_before, part))
            finish(roll_before, pieces)

        cross_fetch.wait()
        fetch(1, 1).start()
        fetch(2, 2).start()
        cross_lanes = jnp.concatenate([cross[...].astype(jnp.float32)] * groups, axis=0).T
        lane_group = lax.broadcasted_iota(jnp.int32, (depth, LANES), 1) // rank
        blank = jnp.zeros((depth, LANES), jnp.bfloat16)
        for tile in range(tiles):
            near, far = tile % 2 * LANES, (1 - tile % 2) * LANES
            placed = jnp.where(lane_group == tile // 2, cross_lanes, 0.0).astype(jnp.bfloat16)
            weights[tile, :, near : near + LANES] = placed
            weights[tile, :, far : far + LANES] = blank
        mach_fetch.wait()
        fetch(3, 3).start()
        spread[...] = jnp.concatenate(
            [mach[:, group * span : (group + 1) * span].astype(jnp.float32) for group in range(groups)], axis=0
        ).T

        for part in range(parts):
            collect(0, 0, part)
        for unit in range(UNITS):
            pltpu.matmul_pop(gram_sums[unit])

        mach_rows[...] = jnp.zeros_like(mach_rows)
        mach_rows[rank : 2 * rank, :] = mach[...]
        cross_rows[...] = jnp.zeros_like(cross_rows)
        cross_rows[2 * rank : 3 * rank, :] = cross[...]
        work = [(mach_rows, mach, first) for first in range(0, bins, WIDE)]
        work += [(cross_rows, cross, first) for first in range(0, depth, WIDE)]
        for count, (right, left, first) in enumerate(work):
            unit, stage = count % UNITS, count // UNITS % 2
            pltpu.matmul_push_rhs(right[:, first : first + WIDE], stage, unit, transpose=True)
            pltpu.matmul_acc_lhs(gram_sums[unit], left[:, first : first + WIDE], load_staged_rhs=stage)
        grams[...] = (pltpu.matmul_pop(gram_sums[0]) + pltpu.matmul_pop(gram_sums[1]))[:, 0:LANES]

        def two_rolls(step, carry):
            roll = 2 * step
            slot = lax.rem(roll, slots)

            @pl.when(roll + ahead < rolls)
            def _():
                next_slot = lax.rem(roll + ahead, slots)
                fetch(roll + ahead, next_slot).start()
                fetch(roll + ahead + 1, next_slot + 1).start()

            fetch(roll, slot).wait()
            one_roll(0, slot, jnp.maximum(roll - 1, 0))
            fetch(roll + 1, slot + 1).wait()
            one_roll(1, slot + 1, roll)
            return carry

        lax.fori_loop(0, rolls // 2, two_rolls, 0)
        finish(rolls - 1, [collect(1, rolls - 1, part) for part in range(parts)])

    pl.run_scoped(
        multiply,
        *[pltpu.ACC(unit)((part_rows, WIDE), jnp.float32) for _ in range(2) for unit in range(UNITS) for _ in range(parts)],
        *[pltpu.ACC(unit)((rank, WIDE), jnp.float32) for unit in range(UNITS)],
    )

    summed = terms[:, 0:rank]
    for group in range(1, groups):
        summed = summed + terms[:, group * rank : (group + 1) * rank]
    payload[...] = grams[...]
    payload[:, 0:rank] = summed


def stream(density, mach, cross):
    rolls, bins, depth = density.shape
    rank = cross.shape[0]
    groups = LANES // rank
    span = bins // groups
    slots = 8
    assert rolls == rank and depth == UNITS * WIDE
    in_hbm = functools.partial(pltpu.with_memory_space_constraint, memory_space=pltpu.HBM)
    anywhere = pl.BlockSpec(memory_space=pl.ANY)
    vmem = pl.BlockSpec(memory_space=pltpu.VMEM)
    return pl.pallas_call(
        stream_kernel,
        out_shape=(
            pltpu.VMEM((rolls, span, LANES), jnp.float32),
            pltpu.VMEM((rolls, LANES), jnp.float32),
        ),
        in_specs=[anywhere, anywhere, anywhere],
        out_specs=(vmem, vmem),
        scratch_shapes=[
            pltpu.VMEM((slots, bins, depth), jnp.bfloat16),
            pltpu.VMEM(mach.shape, mach.dtype),
            pltpu.VMEM(cross.shape, cross.dtype),
            pltpu.VMEM((2 * groups, depth, WIDE), jnp.bfloat16),
            pltpu.VMEM((span, LANES), jnp.float32),
            pltpu.VMEM((rolls, LANES), jnp.float32),
            pltpu.VMEM((WIDE, bins), jnp.bfloat16),
            pltpu.VMEM((WIDE, depth), jnp.bfloat16),
            pltpu.VMEM((rank, LANES), jnp.float32),
            pltpu.SemaphoreType.DMA((slots,)),
            pltpu.SemaphoreType.DMA((2,)),
        ],
        compiler_params=pltpu.CompilerParams(vmem_limit_bytes=40 * MIB),
        cost_estimate=pl.CostEstimate(
            flops=2 * rolls * bins * depth * rank, bytes_accessed=2 * rolls * bins * depth, transcendentals=0
        ),
        name="stream",
    )(density, in_hbm(mach), in_hbm(cross))


def update_kernel(scale, partial, payload, start, roll_out, keep, send, total, blocks, roll_rows, share_wide):
    rolls, span, lanes = partial.shape
    rank = start.shape[0]
    groups = lanes // rank
    half = rank // 2
    flipped = payload[...].T
    gram = flipped[rank : 2 * rank] * flipped[2 * rank : 3 * rank]
    row_id = lax.broadcasted_iota(jnp.int32, (rank, rank), 0)
    lane_id = lax.broadcasted_iota(jnp.int32, (rank, rank), 1)
    diag = jnp.sum(jnp.where(row_id == lane_id, gram, 0.0), axis=1, keepdims=True)
    share = gram / diag
    rows = start[...]
    upper = jnp.where(lane_id > row_id, share, 0.0)
    scaled = flipped[0:rank] / diag
    for r in range(rank):
        share_wide[r] = jnp.broadcast_to(share[:, r : r + 1], (rank, rolls))
    old = jnp.dot(upper, rows, precision=lax.Precision.HIGHEST, preferred_element_type=jnp.float32)
    roll_rows[...] = scaled - old
    gap = [roll_rows[r : r + 1, :] for r in range(rank)]
    done = []
    for r in range(rank):
        updated = jnp.maximum(gap[r], 0.0)
        for later in range(r + 1, rank):
            gap[later] = gap[later] - share_wide[r, later : later + 1, :] * updated
        done.append(updated)
    factor = jnp.concatenate(done, axis=0)
    roll_out[...] = factor
    factor_lanes = jnp.concatenate([factor * scale] * groups, axis=0).T

    chunk = min(span, 64)
    for first in range(0, span, chunk):
        value = partial[0, first : first + chunk, :] * factor_lanes[0:1, :]
        for roll in range(1, rolls):
            value = value + partial[roll, first : first + chunk, :] * factor_lanes[roll : roll + 1, :]
        total[first : first + chunk, :] = value
    blocks[...] = total[...].T.reshape(groups, 2, half, span)
    core = lax.rem(lax.axis_index("roll"), 2)
    cross_at = lax.axis_index("cross")
    for slot, distance in enumerate((0, 2, 1, 3)):
        keep[slot] = blocks[cross_at ^ distance, core]
        send[slot] = blocks[cross_at ^ distance, 1 - core]

def update(scale, partial, payload, start):
    rolls, span, lanes = partial.shape
    rank = start.shape[0]
    groups = lanes // rank
    vmem = pl.BlockSpec(memory_space=pltpu.VMEM)
    part = pltpu.VMEM((groups, rank // 2, span), jnp.float32)
    return pl.pallas_call(
        functools.partial(update_kernel, scale),
        out_shape=(pltpu.VMEM((rank, rolls), jnp.float32), part, part),
        in_specs=[vmem, vmem, vmem],
        out_specs=(vmem, vmem, vmem),
        scratch_shapes=[
            pltpu.VMEM((span, lanes), jnp.float32),
            pltpu.VMEM((groups, 2, rank // 2, span), jnp.float32),
            pltpu.VMEM((rank, rolls), jnp.float32),
            pltpu.VMEM((rank, rank, rolls), jnp.float32),
        ],
        compiler_params=pltpu.CompilerParams(vmem_limit_bytes=40 * MIB),
        cost_estimate=pl.CostEstimate(flops=4 * rolls * span * lanes, bytes_accessed=0, transcendentals=0),
        name="update",
    )(pltpu.with_memory_space_constraint(partial, pltpu.VMEM), payload, start)


def swap(value, axes, distance):
    axes = axes if isinstance(axes, tuple) else (axes,)
    count = 1
    for axis in axes:
        count *= lax.axis_size(axis)
    return lax.ppermute(value, axes, [(source, source ^ distance) for source in range(count)])


def reduce_payload(payload, rank):
    mach_size, cross_size = lax.axis_size("mach"), lax.axis_size("cross")
    lane = lax.broadcasted_iota(jnp.int32, payload.shape, 1)
    is_term = lane < rank
    is_mach = jnp.logical_and(lane >= rank, lane < 2 * rank)
    is_cross = jnp.logical_and(lane >= 2 * rank, lane < 3 * rank)

    both = ("mach", "cross")
    over_mach = swap(payload, both, cross_size)
    over_cross = swap(payload, both, 1)
    over_both = swap(payload, both, cross_size + 1)
    payload = payload + (
        jnp.where(jnp.logical_or(is_term, is_mach), over_mach, 0.0)
        + jnp.where(jnp.logical_or(is_term, is_cross), over_cross, 0.0)
        + jnp.where(is_term, over_both, 0.0)
    )
    distance = 2
    while distance < mach_size:
        arrived = swap(payload, "mach", distance)
        payload = payload + jnp.where(is_cross, 0.0, arrived)
        distance *= 2
    distance = 2
    while distance < cross_size:
        arrived = swap(payload, "cross", distance)
        payload = payload + jnp.where(is_mach, 0.0, arrived)
        distance *= 2
    return payload


def reduce_blocks(keep, send):
    cross_size = lax.axis_size("cross")
    value = keep + swap(send, "roll", 1)
    mine, his = value[:2], value[2:]
    by_cross = swap(his, "cross", 1)
    by_roll = swap(mine, "roll", 2)
    by_both = swap(his, ("roll", "cross"), 2 * cross_size + 1)
    value = mine + (by_cross + (by_roll + by_both))
    value = value[0] + swap(value[1], "cross", 2)
    return value, swap(value, "roll", 1)


def join_kernel(own, other, factor, factor_out, out, sem):
    core = lax.rem(lax.axis_index("roll"), 2)
    half = own.shape[0]
    stores = (
        pltpu.make_async_copy(own, out.at[pl.ds(pl.multiple_of(core * half, half), half)], sem.at[0]),
        pltpu.make_async_copy(other, out.at[pl.ds(pl.multiple_of((1 - core) * half, half), half)], sem.at[1]),
        pltpu.make_async_copy(factor, factor_out, sem.at[2]),
    )
    for store in stores:
        store.start()
    for store in stores:
        store.wait()


def join(own, other, factor):
    vmem = pl.BlockSpec(memory_space=pltpu.VMEM)
    anywhere = pl.BlockSpec(memory_space=pl.ANY)
    return pl.pallas_call(
        join_kernel,
        out_shape=(
            jax.ShapeDtypeStruct(factor.shape, factor.dtype),
            jax.ShapeDtypeStruct((2 * own.shape[0], own.shape[1]), own.dtype),
        ),
        in_specs=[vmem, vmem, vmem],
        out_specs=(anywhere, anywhere),
        scratch_shapes=[pltpu.SemaphoreType.DMA((3,))],
        compiler_params=pltpu.CompilerParams(vmem_limit_bytes=8 * MIB),
        name="join",
    )(own, other, factor)


def local(density, roll_start, mach_factor, cross_factor):
    rolls_here, _, cross_here = density.shape
    rank = cross_factor.shape[0]
    all_rolls = rolls_here * lax.axis_size("roll")
    all_cross = cross_here * lax.axis_size("cross")
    scale = rank / (all_rolls * all_cross)
    partial_value, payload = stream(density, mach_factor, cross_factor)
    payload = reduce_payload(payload, rank)
    roll_factor, keep, send = update(scale, partial_value, payload, roll_start)
    own, other = reduce_blocks(keep, send)
    return join(own, other, roll_factor)


def solution(mesh):
    assert mesh.shape["roll"] == 4 and mesh.shape["cross"] == 4
    in_specs = (P("roll", "mach", "cross"), P(None, "roll"), P(None, "mach"), P(None, "cross"))
    out_specs = (P(None, "roll"), P(None, ("mach", "cross")))
    return jax.shard_map(local, mesh=mesh, in_specs=in_specs, out_specs=out_specs, check_vma=False)
```

```python
import functools

import jax
import jax.numpy as jnp
from jax import lax
from jax.experimental import pallas as pl
from jax.experimental.pallas import tpu as pltpu
from jax.sharding import PartitionSpec as P

LANES = 128
MIB = 1024 * 1024
WIDE = 256
UNITS = 2


def stream_kernel(
    density, mach_hbm, cross_hbm, partial, payload,
    block, mach, cross, weights, spread, terms, mach_rows, cross_rows, grams, sem, factor_sem,
):
    rolls, bins, depth = density.shape
    rank = cross.shape[0]
    groups = LANES // rank
    span = bins // groups
    slots = block.shape[0]
    ahead = 4
    tiles = 2 * groups
    tile_rows = span // 2
    part_rows = min(tile_rows, 128)
    parts = tile_rows // part_rows

    def fetch(roll, slot):
        return pltpu.make_async_copy(density.at[roll], block.at[slot], sem.at[slot])

    cross_fetch = pltpu.make_async_copy(cross_hbm, cross, factor_sem.at[0])
    mach_fetch = pltpu.make_async_copy(mach_hbm, mach, factor_sem.at[1])
    cross_fetch.start()
    mach_fetch.start()
    fetch(0, 0).start()

    def multiply(*sums):
        turns, gram_sums = sums[:-UNITS], sums[-UNITS:]

        def sum_of(turn, unit, part):
            return turns[(turn * UNITS + unit) * parts + part]

        def issue(turn, slot, tile):
            for unit in range(UNITS):
                pltpu.matmul_push_rhs(weights[tile, unit * WIDE : (unit + 1) * WIDE, :], tile % 2, unit)
            for part in range(parts):
                first = tile * tile_rows + part * part_rows
                for unit in range(UNITS):
                    pltpu.matmul_acc_lhs(
                        sum_of(turn, unit, part),
                        block[slot, first : first + part_rows, unit * WIDE : (unit + 1) * WIDE],
                        load_staged_rhs=tile % 2 if part == 0 else None,
                    )

        def collect(turn, roll, part):
            value = pltpu.matmul_pop(sum_of(turn, 0, part)) + pltpu.matmul_pop(sum_of(turn, 1, part))
            total = None
            for half in range(2):
                first = half * tile_rows + part * part_rows
                piece = value[:, half * LANES : (half + 1) * LANES]
                partial[roll, first : first + part_rows, :] = piece
                weighted = piece * spread[first : first + part_rows, :]
                total = weighted if total is None else total + weighted
            return jnp.sum(total, axis=0, keepdims=True)

        def finish(roll, pieces):
            terms[pl.ds(roll, 1), :] = sum(pieces[1:], pieces[0])

        def one_roll(turn, slot, roll_before):
            pieces = []
            for tile in range(tiles):
                issue(turn, slot, tile)
                for part in range(tile * parts // tiles, (tile + 1) * parts // tiles):
                    pieces.append(collect(1 - turn, roll_before, part))
            finish(roll_before, pieces)

        cross_fetch.wait()
        fetch(1, 1).start()
        fetch(2, 2).start()
        cross_lanes = jnp.concatenate([cross[...].astype(jnp.float32)] * groups, axis=0).T
        lane_group = lax.broadcasted_iota(jnp.int32, (depth, LANES), 1) // rank
        blank = jnp.zeros((depth, LANES), jnp.bfloat16)
        for tile in range(tiles):
            near, far = tile % 2 * LANES, (1 - tile % 2) * LANES
            placed = jnp.where(lane_group == tile // 2, cross_lanes, 0.0).astype(jnp.bfloat16)
            weights[tile, :, near : near + LANES] = placed
            weights[tile, :, far : far + LANES] = blank
        mach_fetch.wait()
        fetch(3, 3).start()
        spread[...] = jnp.concatenate(
            [mach[:, group * span : (group + 1) * span].astype(jnp.float32) for group in range(groups)], axis=0
        ).T

        for part in range(parts):
            collect(0, 0, part)
        for unit in range(UNITS):
            pltpu.matmul_pop(gram_sums[unit])

        mach_rows[...] = jnp.zeros_like(mach_rows)
        mach_rows[rank : 2 * rank, :] = mach[...]
        cross_rows[...] = jnp.zeros_like(cross_rows)
        cross_rows[2 * rank : 3 * rank, :] = cross[...]
        work = [(mach_rows, mach, first) for first in range(0, bins, WIDE)]
        work += [(cross_rows, cross, first) for first in range(0, depth, WIDE)]
        for count, (right, left, first) in enumerate(work):
            unit, stage = count % UNITS, count // UNITS % 2
            pltpu.matmul_push_rhs(right[:, first : first + WIDE], stage, unit, transpose=True)
            pltpu.matmul_acc_lhs(gram_sums[unit], left[:, first : first + WIDE], load_staged_rhs=stage)
        grams[...] = (pltpu.matmul_pop(gram_sums[0]) + pltpu.matmul_pop(gram_sums[1]))[:, 0:LANES]

        def two_rolls(step, carry):
            roll = 2 * step
            slot = lax.rem(roll, slots)

            @pl.when(roll + ahead < rolls)
            def _():
                next_slot = lax.rem(roll + ahead, slots)
                fetch(roll + ahead, next_slot).start()
                fetch(roll + ahead + 1, next_slot + 1).start()

            fetch(roll, slot).wait()
            one_roll(0, slot, jnp.maximum(roll - 1, 0))
            fetch(roll + 1, slot + 1).wait()
            one_roll(1, slot + 1, roll)
            return carry

        lax.fori_loop(0, rolls // 2, two_rolls, 0)
        finish(rolls - 1, [collect(1, rolls - 1, part) for part in range(parts)])

    pl.run_scoped(
        multiply,
        *[pltpu.ACC(unit)((part_rows, WIDE), jnp.float32) for _ in range(2) for unit in range(UNITS) for _ in range(parts)],
        *[pltpu.ACC(unit)((rank, WIDE), jnp.float32) for unit in range(UNITS)],
    )

    summed = terms[:, 0:rank]
    for group in range(1, groups):
        summed = summed + terms[:, group * rank : (group + 1) * rank]
    payload[...] = grams[...]
    payload[:, 0:rank] = summed


def stream(density, mach, cross):
    rolls, bins, depth = density.shape
    rank = cross.shape[0]
    groups = LANES // rank
    span = bins // groups
    slots = 8
    assert rolls == rank and depth == UNITS * WIDE
    in_hbm = functools.partial(pltpu.with_memory_space_constraint, memory_space=pltpu.HBM)
    anywhere = pl.BlockSpec(memory_space=pl.ANY)
    vmem = pl.BlockSpec(memory_space=pltpu.VMEM)
    return pl.pallas_call(
        stream_kernel,
        out_shape=(
            pltpu.VMEM((rolls, span, LANES), jnp.float32),
            pltpu.VMEM((rolls, LANES), jnp.float32),
        ),
        in_specs=[anywhere, anywhere, anywhere],
        out_specs=(vmem, vmem),
        scratch_shapes=[
            pltpu.VMEM((slots, bins, depth), jnp.bfloat16),
            pltpu.VMEM(mach.shape, mach.dtype),
            pltpu.VMEM(cross.shape, cross.dtype),
            pltpu.VMEM((2 * groups, depth, WIDE), jnp.bfloat16),
            pltpu.VMEM((span, LANES), jnp.float32),
            pltpu.VMEM((rolls, LANES), jnp.float32),
            pltpu.VMEM((WIDE, bins), jnp.bfloat16),
            pltpu.VMEM((WIDE, depth), jnp.bfloat16),
            pltpu.VMEM((rank, LANES), jnp.float32),
            pltpu.SemaphoreType.DMA((slots,)),
            pltpu.SemaphoreType.DMA((2,)),
        ],
        compiler_params=pltpu.CompilerParams(vmem_limit_bytes=40 * MIB),
        cost_estimate=pl.CostEstimate(
            flops=2 * rolls * bins * depth * rank, bytes_accessed=2 * rolls * bins * depth, transcendentals=0
        ),
        name="stream",
    )(density, in_hbm(mach), in_hbm(cross))


def half_term(partial, factor_lanes, half, out, total, blocks):
    rolls, span, _ = partial.shape
    groups, rank, bins = blocks.shape
    chunk = min(bins, 64)
    for first in range(0, bins, chunk):
        rows = pl.ds(pl.multiple_of(half * bins + first, chunk), chunk)
        value = partial[0, rows, :] * factor_lanes[0:1, :]
        for roll in range(1, rolls):
            value = value + partial[roll, rows, :] * factor_lanes[roll : roll + 1, :]
        total[first : first + chunk, :] = value
    blocks[...] = total[...].T.reshape(groups, rank, bins)
    cross_at = lax.axis_index("cross")
    for slot, distance in enumerate((0, 2, 1, 3)):
        out[slot] = blocks[cross_at ^ distance]


def this_core():
    return lax.rem(lax.axis_index("roll"), 2)


def update_kernel(
    scale, partial, payload, start, roll_out, lanes_out, send, total, blocks, roll_rows, share_wide
):
    rolls, span, lanes = partial.shape
    rank = start.shape[0]
    groups = lanes // rank
    flipped = payload[...].T
    gram = flipped[rank : 2 * rank] * flipped[2 * rank : 3 * rank]
    row_id = lax.broadcasted_iota(jnp.int32, (rank, rank), 0)
    lane_id = lax.broadcasted_iota(jnp.int32, (rank, rank), 1)
    diag = jnp.sum(jnp.where(row_id == lane_id, gram, 0.0), axis=1, keepdims=True)
    share = gram / diag
    rows = start[...]
    upper = jnp.where(lane_id > row_id, share, 0.0)
    scaled = flipped[0:rank] / diag
    for r in range(rank):
        share_wide[r] = jnp.broadcast_to(share[:, r : r + 1], (rank, rolls))
    old = jnp.dot(upper, rows, precision=lax.Precision.HIGHEST, preferred_element_type=jnp.float32)
    roll_rows[...] = scaled - old
    gap = [roll_rows[r : r + 1, :] for r in range(rank)]
    done = []
    for r in range(rank):
        updated = jnp.maximum(gap[r], 0.0)
        for later in range(r + 1, rank):
            gap[later] = gap[later] - share_wide[r, later : later + 1, :] * updated
        done.append(updated)
    factor = jnp.concatenate(done, axis=0)
    roll_out[...] = factor
    factor_lanes = jnp.concatenate([factor * scale] * groups, axis=0).T
    lanes_out[...] = factor_lanes
    half_term(partial, factor_lanes, 1 - this_core(), send, total, blocks)


def keep_kernel(partial, factor_lanes, keep, total, blocks):
    half_term(partial, factor_lanes[...], this_core(), keep, total, blocks)


def update(scale, partial, payload, start):
    rolls, span, lanes = partial.shape
    rank = start.shape[0]
    vmem = pl.BlockSpec(memory_space=pltpu.VMEM)
    in_vmem = functools.partial(pltpu.with_memory_space_constraint, memory_space=pltpu.VMEM)
    partial = in_vmem(partial)
    part = pltpu.VMEM((lanes // rank, rank, span // 2), jnp.float32)
    work = [
        pltpu.VMEM((span // 2, lanes), jnp.float32),
        pltpu.VMEM((lanes // rank, rank, span // 2), jnp.float32),
    ]
    cost = pl.CostEstimate(flops=rolls * span * lanes, bytes_accessed=0, transcendentals=0)
    roll_factor, factor_lanes, send = pl.pallas_call(
        functools.partial(update_kernel, scale),
        out_shape=(
            pltpu.VMEM((rank, rolls), jnp.float32),
            pltpu.VMEM((rolls, lanes), jnp.float32),
            part,
        ),
        in_specs=[vmem, vmem, vmem],
        out_specs=(vmem, vmem, vmem),
        scratch_shapes=work
        + [pltpu.VMEM((rank, rolls), jnp.float32), pltpu.VMEM((rank, rank, rolls), jnp.float32)],
        compiler_params=pltpu.CompilerParams(vmem_limit_bytes=40 * MIB),
        cost_estimate=cost,
        name="update",
    )(partial, in_vmem(payload), start)
    from_core = swap(send, "roll", 1)
    keep = pl.pallas_call(
        keep_kernel,
        out_shape=part,
        in_specs=[vmem, vmem],
        out_specs=vmem,
        scratch_shapes=work,
        compiler_params=pltpu.CompilerParams(vmem_limit_bytes=40 * MIB),
        cost_estimate=cost,
        name="keep",
    )(partial, in_vmem(factor_lanes))
    return roll_factor, keep, from_core


def swap(value, axes, distance):
    axes = axes if isinstance(axes, tuple) else (axes,)
    count = 1
    for axis in axes:
        count *= lax.axis_size(axis)
    return lax.ppermute(value, axes, [(source, source ^ distance) for source in range(count)])


def reduce_payload(payload, rank):
    mach_size, cross_size = lax.axis_size("mach"), lax.axis_size("cross")
    lane = lax.broadcasted_iota(jnp.int32, payload.shape, 1)
    is_term = lane < rank
    is_mach = jnp.logical_and(lane >= rank, lane < 2 * rank)
    is_cross = jnp.logical_and(lane >= 2 * rank, lane < 3 * rank)

    both = ("mach", "cross")
    over_mach = swap(payload, both, cross_size)
    over_cross = swap(payload, both, 1)
    over_both = swap(payload, both, cross_size + 1)
    payload = payload + (
        jnp.where(jnp.logical_or(is_term, is_mach), over_mach, 0.0)
        + jnp.where(jnp.logical_or(is_term, is_cross), over_cross, 0.0)
        + jnp.where(is_term, over_both, 0.0)
    )
    distance = 2
    while distance < mach_size:
        arrived = swap(payload, "mach", distance)
        payload = payload + jnp.where(is_cross, 0.0, arrived)
        distance *= 2
    distance = 2
    while distance < cross_size:
        arrived = swap(payload, "cross", distance)
        payload = payload + jnp.where(is_mach, 0.0, arrived)
        distance *= 2
    return payload


def reduce_blocks(keep, from_core):
    cross_size = lax.axis_size("cross")
    value = keep + from_core
    mine, his = value[:2], value[2:]
    by_cross = swap(his, "cross", 1)
    by_roll = swap(mine, "roll", 2)
    by_both = swap(his, ("roll", "cross"), 2 * cross_size + 1)
    value = mine + (by_cross + (by_roll + by_both))
    value = value[0] + swap(value[1], "cross", 2)
    return value, swap(value, "roll", 1)


def join_kernel(own, other, factor, factor_out, out, whole, sem):
    core = this_core()
    bins = own.shape[1]
    if bins % LANES:
        both = jnp.concatenate([own[...], other[...]], axis=1)
        turned = jnp.concatenate([other[...], own[...]], axis=1)
        whole[...] = jnp.where(core == 0, both, turned)
        stores = (pltpu.make_async_copy(whole, out, sem.at[0]),)
    else:
        stores = (
            pltpu.make_async_copy(own, out.at[:, pl.ds(pl.multiple_of(core * bins, bins), bins)], sem.at[0]),
            pltpu.make_async_copy(other, out.at[:, pl.ds(pl.multiple_of((1 - core) * bins, bins), bins)], sem.at[1]),
        )
    stores += (pltpu.make_async_copy(factor, factor_out, sem.at[2]),)
    for store in stores:
        store.start()
    for store in stores:
        store.wait()


def join(own, other, factor):
    vmem = pl.BlockSpec(memory_space=pltpu.VMEM)
    anywhere = pl.BlockSpec(memory_space=pl.ANY)
    return pl.pallas_call(
        join_kernel,
        out_shape=(
            jax.ShapeDtypeStruct(factor.shape, factor.dtype),
            jax.ShapeDtypeStruct((own.shape[0], 2 * own.shape[1]), own.dtype),
        ),
        in_specs=[vmem, vmem, vmem],
        out_specs=(anywhere, anywhere),
        scratch_shapes=[
            pltpu.VMEM((own.shape[0], 2 * own.shape[1]), own.dtype),
            pltpu.SemaphoreType.DMA((3,)),
        ],
        compiler_params=pltpu.CompilerParams(vmem_limit_bytes=8 * MIB),
        name="join",
    )(own, other, factor)


def local(density, roll_start, mach_factor, cross_factor):
    rolls_here, _, cross_here = density.shape
    rank = cross_factor.shape[0]
    all_rolls = rolls_here * lax.axis_size("roll")
    all_cross = cross_here * lax.axis_size("cross")
    scale = rank / (all_rolls * all_cross)
    partial_value, payload = stream(density, mach_factor, cross_factor)
    payload = reduce_payload(payload, rank)
    roll_factor, keep, from_core = update(scale, partial_value, payload, roll_start)
    own, other = reduce_blocks(keep, from_core)
    return join(own, other, roll_factor)


def solution(mesh):
    assert mesh.shape["roll"] == 4 and mesh.shape["cross"] == 4
    in_specs = (P("roll", "mach", "cross"), P(None, "roll"), P(None, "mach"), P(None, "cross"))
    out_specs = (P(None, "roll"), P(None, ("mach", "cross")))
    return jax.shard_map(local, mesh=mesh, in_specs=in_specs, out_specs=out_specs, check_vma=False)
```

```python
import functools

import jax
import jax.numpy as jnp
from jax import lax
from jax.experimental import pallas as pl
from jax.experimental.pallas import tpu as pltpu
from jax.sharding import PartitionSpec as P

LANES = 128
MIB = 1024 * 1024
WIDE = 256
UNITS = 2


def stream_kernel(
    density, mach_hbm, cross_hbm, partial, payload,
    block, mach, cross, weights, spread, terms, mach_rows, cross_rows, grams, sem, factor_sem,
):
    rolls, bins, depth = density.shape
    rank = cross.shape[0]
    groups = LANES // rank
    span = bins // groups
    slots = block.shape[0]
    ahead = 4
    tiles = 2 * groups
    tile_rows = span // 2
    part_rows = min(tile_rows, 128)
    parts = tile_rows // part_rows

    def fetch(roll, slot):
        return pltpu.make_async_copy(density.at[roll], block.at[slot], sem.at[slot])

    cross_fetch = pltpu.make_async_copy(cross_hbm, cross, factor_sem.at[0])
    mach_fetch = pltpu.make_async_copy(mach_hbm, mach, factor_sem.at[1])
    cross_fetch.start()
    mach_fetch.start()
    fetch(0, 0).start()

    def multiply(*sums):
        turns, gram_sums = sums[:-UNITS], sums[-UNITS:]

        def sum_of(turn, unit, part):
            return turns[(turn * UNITS + unit) * parts + part]

        def issue(turn, slot, tile):
            for unit in range(UNITS):
                pltpu.matmul_push_rhs(weights[tile, unit * WIDE : (unit + 1) * WIDE, :], tile % 2, unit)
            for part in range(parts):
                first = tile * tile_rows + part * part_rows
                for unit in range(UNITS):
                    pltpu.matmul_acc_lhs(
                        sum_of(turn, unit, part),
                        block[slot, first : first + part_rows, unit * WIDE : (unit + 1) * WIDE],
                        load_staged_rhs=tile % 2 if part == 0 else None,
                    )

        def collect(turn, roll, part):
            value = pltpu.matmul_pop(sum_of(turn, 0, part)) + pltpu.matmul_pop(sum_of(turn, 1, part))
            total = None
            for half in range(2):
                first = half * tile_rows + part * part_rows
                piece = value[:, half * LANES : (half + 1) * LANES]
                partial[roll, first : first + part_rows, :] = piece
                weighted = piece * spread[first : first + part_rows, :]
                total = weighted if total is None else total + weighted
            return jnp.sum(total, axis=0, keepdims=True)

        def finish(roll, pieces):
            terms[pl.ds(roll, 1), :] = sum(pieces[1:], pieces[0])

        def one_roll(turn, slot, roll_before):
            pieces = []
            for tile in range(tiles):
                issue(turn, slot, tile)
                for part in range(tile * parts // tiles, (tile + 1) * parts // tiles):
                    pieces.append(collect(1 - turn, roll_before, part))
            finish(roll_before, pieces)

        cross_fetch.wait()
        fetch(1, 1).start()
        fetch(2, 2).start()
        cross_lanes = jnp.concatenate([cross[...].astype(jnp.float32)] * groups, axis=0).T
        lane_group = lax.broadcasted_iota(jnp.int32, (depth, LANES), 1) // rank
        blank = jnp.zeros((depth, LANES), jnp.bfloat16)
        for tile in range(tiles):
            near, far = tile % 2 * LANES, (1 - tile % 2) * LANES
            placed = jnp.where(lane_group == tile // 2, cross_lanes, 0.0).astype(jnp.bfloat16)
            weights[tile, :, near : near + LANES] = placed
            weights[tile, :, far : far + LANES] = blank
        mach_fetch.wait()
        fetch(3, 3).start()
        spread[...] = jnp.concatenate(
            [mach[:, group * span : (group + 1) * span].astype(jnp.float32) for group in range(groups)], axis=0
        ).T

        for part in range(parts):
            collect(0, 0, part)
        for unit in range(UNITS):
            pltpu.matmul_pop(gram_sums[unit])

        mach_rows[...] = jnp.zeros_like(mach_rows)
        mach_rows[rank : 2 * rank, :] = mach[...]
        cross_rows[...] = jnp.zeros_like(cross_rows)
        cross_rows[2 * rank : 3 * rank, :] = cross[...]
        work = [(mach_rows, mach, first) for first in range(0, bins, WIDE)]
        work += [(cross_rows, cross, first) for first in range(0, depth, WIDE)]
        for count, (right, left, first) in enumerate(work):
            unit, stage = count % UNITS, count // UNITS % 2
            pltpu.matmul_push_rhs(right[:, first : first + WIDE], stage, unit, transpose=True)
            pltpu.matmul_acc_lhs(gram_sums[unit], left[:, first : first + WIDE], load_staged_rhs=stage)
        grams[...] = (pltpu.matmul_pop(gram_sums[0]) + pltpu.matmul_pop(gram_sums[1]))[:, 0:LANES]

        def two_rolls(step, carry):
            roll = 2 * step
            slot = lax.rem(roll, slots)

            @pl.when(roll + ahead < rolls)
            def _():
                next_slot = lax.rem(roll + ahead, slots)
                fetch(roll + ahead, next_slot).start()
                fetch(roll + ahead + 1, next_slot + 1).start()

            fetch(roll, slot).wait()
            one_roll(0, slot, jnp.maximum(roll - 1, 0))
            fetch(roll + 1, slot + 1).wait()
            one_roll(1, slot + 1, roll)
            return carry

        lax.fori_loop(0, rolls // 2, two_rolls, 0)
        finish(rolls - 1, [collect(1, rolls - 1, part) for part in range(parts)])

    pl.run_scoped(
        multiply,
        *[pltpu.ACC(unit)((part_rows, WIDE), jnp.float32) for _ in range(2) for unit in range(UNITS) for _ in range(parts)],
        *[pltpu.ACC(unit)((rank, WIDE), jnp.float32) for unit in range(UNITS)],
    )

    summed = terms[:, 0:rank]
    for group in range(1, groups):
        summed = summed + terms[:, group * rank : (group + 1) * rank]
    payload[...] = grams[...]
    payload[:, 0:rank] = summed


def stream(density, mach, cross):
    rolls, bins, depth = density.shape
    rank = cross.shape[0]
    groups = LANES // rank
    span = bins // groups
    slots = 8
    assert rolls == rank and depth == UNITS * WIDE
    in_hbm = functools.partial(pltpu.with_memory_space_constraint, memory_space=pltpu.HBM)
    anywhere = pl.BlockSpec(memory_space=pl.ANY)
    vmem = pl.BlockSpec(memory_space=pltpu.VMEM)
    return pl.pallas_call(
        stream_kernel,
        out_shape=(
            pltpu.VMEM((rolls, span, LANES), jnp.float32),
            pltpu.VMEM((rolls, LANES), jnp.float32),
        ),
        in_specs=[anywhere, anywhere, anywhere],
        out_specs=(vmem, vmem),
        scratch_shapes=[
            pltpu.VMEM((slots, bins, depth), jnp.bfloat16),
            pltpu.VMEM(mach.shape, mach.dtype),
            pltpu.VMEM(cross.shape, cross.dtype),
            pltpu.VMEM((2 * groups, depth, WIDE), jnp.bfloat16),
            pltpu.VMEM((span, LANES), jnp.float32),
            pltpu.VMEM((rolls, LANES), jnp.float32),
            pltpu.VMEM((WIDE, bins), jnp.bfloat16),
            pltpu.VMEM((WIDE, depth), jnp.bfloat16),
            pltpu.VMEM((rank, LANES), jnp.float32),
            pltpu.SemaphoreType.DMA((slots,)),
            pltpu.SemaphoreType.DMA((2,)),
        ],
        compiler_params=pltpu.CompilerParams(vmem_limit_bytes=40 * MIB),
        cost_estimate=pl.CostEstimate(
            flops=2 * rolls * bins * depth * rank, bytes_accessed=2 * rolls * bins * depth, transcendentals=0
        ),
        name="stream",
    )(density, in_hbm(mach), in_hbm(cross))


def half_term(partial, factor_lanes, half, out, total, blocks):
    rolls, span, _ = partial.shape
    groups, rank, bins = blocks.shape
    chunk = min(bins, 64)
    for first in range(0, bins, chunk):
        rows = pl.ds(pl.multiple_of(half * bins + first, chunk), chunk)
        value = partial[0, rows, :] * factor_lanes[0:1, :]
        for roll in range(1, rolls):
            value = value + partial[roll, rows, :] * factor_lanes[roll : roll + 1, :]
        total[first : first + chunk, :] = value
    blocks[...] = total[...].T.reshape(groups, rank, bins)
    cross_at = lax.axis_index("cross")
    for slot, distance in enumerate((0, 2, 1, 3)):
        out[slot] = blocks[cross_at ^ distance]


def this_half():
    chip, core = lax.axis_index("roll") // 2, lax.rem(lax.axis_index("roll"), 2)
    cross_at = lax.axis_index("cross")
    return core ^ chip ^ lax.rem(cross_at, 2) ^ (cross_at // 2)


def update_kernel(
    scale, partial, payload, start, roll_out, lanes_out, send, total, blocks, roll_rows, share_wide
):
    rolls, span, lanes = partial.shape
    rank = start.shape[0]
    groups = lanes // rank
    flipped = payload[...].T
    gram = flipped[rank : 2 * rank] * flipped[2 * rank : 3 * rank]
    row_id = lax.broadcasted_iota(jnp.int32, (rank, rank), 0)
    lane_id = lax.broadcasted_iota(jnp.int32, (rank, rank), 1)
    diag = jnp.sum(jnp.where(row_id == lane_id, gram, 0.0), axis=1, keepdims=True)
    share = gram / diag
    rows = start[...]
    upper = jnp.where(lane_id > row_id, share, 0.0)
    scaled = flipped[0:rank] / diag
    for r in range(rank):
        share_wide[r] = jnp.broadcast_to(share[:, r : r + 1], (rank, rolls))
    old = jnp.dot(upper, rows, precision=lax.Precision.HIGHEST, preferred_element_type=jnp.float32)
    roll_rows[...] = scaled - old
    gap = [roll_rows[r : r + 1, :] for r in range(rank)]
    done = []
    for r in range(rank):
        updated = jnp.maximum(gap[r], 0.0)
        for later in range(r + 1, rank):
            gap[later] = gap[later] - share_wide[r, later : later + 1, :] * updated
        done.append(updated)
    factor = jnp.concatenate(done, axis=0)
    roll_out[...] = factor
    factor_lanes = jnp.concatenate([factor * scale] * groups, axis=0).T
    lanes_out[...] = factor_lanes
    half_term(partial, factor_lanes, 1 - this_half(), send, total, blocks)


def keep_kernel(partial, factor_lanes, keep, total, blocks):
    half_term(partial, factor_lanes[...], this_half(), keep, total, blocks)


def update(scale, partial, payload, start):
    rolls, span, lanes = partial.shape
    rank = start.shape[0]
    vmem = pl.BlockSpec(memory_space=pltpu.VMEM)
    in_vmem = functools.partial(pltpu.with_memory_space_constraint, memory_space=pltpu.VMEM)
    partial = in_vmem(partial)
    part = pltpu.VMEM((lanes // rank, rank, span // 2), jnp.float32)
    work = [
        pltpu.VMEM((span // 2, lanes), jnp.float32),
        pltpu.VMEM((lanes // rank, rank, span // 2), jnp.float32),
    ]
    cost = pl.CostEstimate(flops=rolls * span * lanes, bytes_accessed=0, transcendentals=0)
    roll_factor, factor_lanes, send = pl.pallas_call(
        functools.partial(update_kernel, scale),
        out_shape=(
            pltpu.VMEM((rank, rolls), jnp.float32),
            pltpu.VMEM((rolls, lanes), jnp.float32),
            part,
        ),
        in_specs=[vmem, vmem, vmem],
        out_specs=(vmem, vmem, vmem),
        scratch_shapes=work
        + [pltpu.VMEM((rank, rolls), jnp.float32), pltpu.VMEM((rank, rank, rolls), jnp.float32)],
        compiler_params=pltpu.CompilerParams(vmem_limit_bytes=40 * MIB),
        cost_estimate=cost,
        name="update",
    )(partial, in_vmem(payload), start)
    from_core = swap(send, "roll", 1)
    keep = pl.pallas_call(
        keep_kernel,
        out_shape=part,
        in_specs=[vmem, vmem],
        out_specs=vmem,
        scratch_shapes=work,
        compiler_params=pltpu.CompilerParams(vmem_limit_bytes=40 * MIB),
        cost_estimate=cost,
        name="keep",
    )(partial, in_vmem(factor_lanes))
    return roll_factor, keep, from_core


def swap(value, axes, distance):
    axes = axes if isinstance(axes, tuple) else (axes,)
    count = 1
    for axis in axes:
        count *= lax.axis_size(axis)
    return lax.ppermute(value, axes, [(source, source ^ distance) for source in range(count)])


def reduce_payload(payload, rank):
    mach_size, cross_size = lax.axis_size("mach"), lax.axis_size("cross")
    lane = lax.broadcasted_iota(jnp.int32, payload.shape, 1)
    is_term = lane < rank
    is_mach = jnp.logical_and(lane >= rank, lane < 2 * rank)
    is_cross = jnp.logical_and(lane >= 2 * rank, lane < 3 * rank)

    both = ("mach", "cross")
    over_mach = swap(payload, both, cross_size)
    over_cross = swap(payload, both, 1)
    over_both = swap(payload, both, cross_size + 1)
    payload = payload + (
        jnp.where(jnp.logical_or(is_term, is_mach), over_mach, 0.0)
        + jnp.where(jnp.logical_or(is_term, is_cross), over_cross, 0.0)
        + jnp.where(is_term, over_both, 0.0)
    )
    distance = 2
    while distance < mach_size:
        arrived = swap(payload, "mach", distance)
        payload = payload + jnp.where(is_cross, 0.0, arrived)
        distance *= 2
    distance = 2
    while distance < cross_size:
        arrived = swap(payload, "cross", distance)
        payload = payload + jnp.where(is_mach, 0.0, arrived)
        distance *= 2
    return payload


def reduce_blocks(keep, from_core):
    cross_size = lax.axis_size("cross")
    value = keep + from_core
    mine, his = value[:2], value[2:]
    by_cross = swap(his, ("roll", "cross"), 1 * cross_size + 1)
    by_roll = swap(mine, "roll", 3)
    by_both = swap(his, ("roll", "cross"), 2 * cross_size + 1)
    value = mine + (by_cross + (by_roll + by_both))
    value = value[0] + swap(value[1], ("roll", "cross"), 1 * cross_size + 2)
    return value, swap(value, "roll", 1)


def join_kernel(own, other, factor, factor_out, out, whole, sem):
    core = this_half()
    bins = own.shape[1]
    if bins % LANES:
        both = jnp.concatenate([own[...], other[...]], axis=1)
        turned = jnp.concatenate([other[...], own[...]], axis=1)
        whole[...] = jnp.where(core == 0, both, turned)
        stores = (pltpu.make_async_copy(whole, out, sem.at[0]),)
    else:
        stores = (
            pltpu.make_async_copy(own, out.at[:, pl.ds(pl.multiple_of(core * bins, bins), bins)], sem.at[0]),
            pltpu.make_async_copy(other, out.at[:, pl.ds(pl.multiple_of((1 - core) * bins, bins), bins)], sem.at[1]),
        )
    stores += (pltpu.make_async_copy(factor, factor_out, sem.at[2]),)
    for store in stores:
        store.start()
    for store in stores:
        store.wait()


def join(own, other, factor):
    vmem = pl.BlockSpec(memory_space=pltpu.VMEM)
    anywhere = pl.BlockSpec(memory_space=pl.ANY)
    return pl.pallas_call(
        join_kernel,
        out_shape=(
            jax.ShapeDtypeStruct(factor.shape, factor.dtype),
            jax.ShapeDtypeStruct((own.shape[0], 2 * own.shape[1]), own.dtype),
        ),
        in_specs=[vmem, vmem, vmem],
        out_specs=(anywhere, anywhere),
        scratch_shapes=[
            pltpu.VMEM((own.shape[0], 2 * own.shape[1]), own.dtype),
            pltpu.SemaphoreType.DMA((3,)),
        ],
        compiler_params=pltpu.CompilerParams(vmem_limit_bytes=8 * MIB),
        name="join",
    )(own, other, factor)


def local(density, roll_start, mach_factor, cross_factor):
    rolls_here, _, cross_here = density.shape
    rank = cross_factor.shape[0]
    all_rolls = rolls_here * lax.axis_size("roll")
    all_cross = cross_here * lax.axis_size("cross")
    scale = rank / (all_rolls * all_cross)
    partial_value, payload = stream(density, mach_factor, cross_factor)
    payload = reduce_payload(payload, rank)
    roll_factor, keep, from_core = update(scale, partial_value, payload, roll_start)
    own, other = reduce_blocks(keep, from_core)
    return join(own, other, roll_factor)


def solution(mesh):
    assert mesh.shape["roll"] == 4 and mesh.shape["cross"] == 4
    in_specs = (P("roll", "mach", "cross"), P(None, "roll"), P(None, "mach"), P(None, "cross"))
    out_specs = (P(None, "roll"), P(None, ("mach", "cross")))
    return jax.shard_map(local, mesh=mesh, in_specs=in_specs, out_specs=out_specs, check_vma=False)
```
